32 devices in a mesh: grp: 2 (over y), seq: 16 (over z, x, core).
Axes of the slice: x: 2, y: 2, z: 4, core: 2. Of those that a mesh axis runs over, the one named last changes fastest.
Arguments:
- query_input: bfloat16 [4096, 4096], P(('grp', 'seq')), parts along dimension 0, may hold values from -6 to 6
- key_input: bfloat16 [4096, 4096], P(('grp', 'seq')), parts along dimension 0, may hold values from -6 to 6
- value_input: bfloat16 [4096, 4096], P(('grp', 'seq')), parts along dimension 0, may hold values from -6 to 6
- output_grad: bfloat16 [4096, 4096], P(('grp', 'seq')), parts along dimension 0, may hold values from -6 to 6
- short_taps: float32 [3, 7, 4096], replicated, may hold values from -2 to 2
- long_filter: bfloat16 [128, 256], replicated, may hold values from -0.5 to 0.5
- skip_gain: float32 [4096], replicated, may hold values from 0.1 to 1.9
- genome_ids: int32 [4096], P('grp'), parts along dimension 0, may hold values from 0 to 7, never falling along the last dimension, each value on 1 to 512 neighbouring positions
Outputs:
- section_out: bfloat16 [4096, 4096], P(('grp', 'seq')), parts along dimension 0
- grad_query: bfloat16 [4096, 4096], P(('grp', 'seq')), parts along dimension 0
- grad_key: bfloat16 [4096, 4096], P(('grp', 'seq')), parts along dimension 0
- grad_value: bfloat16 [4096, 4096], P(('grp', 'seq')), parts along dimension 0
- filter_grad: float32 [256, 256], P('grp'), parts along dimension 0
The draws below stay inside these ranges and needn't reach their ends.
There are 2 independent parts, one for each index of `grp`. The reference program is written for one: setup_inputs(seed, part) draws one part's arguments, and reference() takes and returns one part's arrays. A program takes and returns all parts, laid end to end along the dimension named above; an argument that names none is the same for every part. Nothing has to cross between parts.
Inputs may be any that keep to these rules, and one draw needn't show every extreme that they name: `genome_ids`: genome ids never fall from one row to the next; each genome covers 1 to 512 rows, one exactly 512.
All inputs are finite; a program needn't handle non-finite values.
Results may differ from the reference program's by a relative error of at most 0.0058.
Values may be sent and summed in bfloat16 or wider, within the bound.
A program may use at most 128 MiB of HBM per device.

```python
import math
import jax
import jax.numpy as jnp
import numpy as np
from jax import lax

W = 4096
GROUP_SIZE = 16
TAPS = 128
SHORT_TAPS = 7
TOKENS = 2048
FILTERS = 256
GENOMES = 8
MOST_LEN = 512


def levels(own_key, extent, cuts, least, largest):
    factor_of, own = 1.0, jax.random.fold_in(own_key, 6)
    for position, shards_of in cuts:
        steps = jnp.exp(jax.random.uniform(jax.random.fold_in(own, position), (shards_of,), jnp.float32, least / len(cuts), largest / len(cuts)))
        factor_of = factor_of * jnp.repeat(steps, extent[position] // shards_of).reshape([-1 if axis == position else 1 for axis in range(len(extent))])
    return factor_of


def split_up(number_of, total, most, lean):
    portions = [(1 << 20) // math.isqrt(grade ** lean) + 1 for grade in range(2, number_of + 1)]
    surplus, counts = total - most - (number_of - 1), [1] * (number_of - 1)
    while surplus > 0:
        free = [i for i in range(number_of - 1) if counts[i] < most]
        mass, budget = sum([portions[i] for i in free]), surplus
        for i in free:
            extra = min(most - counts[i], max(1, budget * portions[i] // mass), surplus)
            counts[i] = counts[i] + extra
            surplus = surplus - extra
    return np.array([most] + counts)


def ragged_sizes(key, number_of, total, reach, slope):
    if number_of == 2:
        one = jax.random.randint(key, (), max(1, total - reach), min(reach, total - 1) + 1)
        return jnp.stack([one, total - one])
    lengths = jnp.asarray(split_up(number_of, total, reach, slope), jnp.int32)
    couples = (number_of - 1) // 2
    source_of, sink = lengths[1:1 + 2 * couples:2], lengths[2:2 + 2 * couples:2]
    margin = jnp.minimum(source_of - 1, reach - sink)
    shifted = jax.random.randint(jax.random.fold_in(key, 1), (couples,), 0, 1 << 20) % (margin + 1)
    lengths = lengths.at[1:1 + 2 * couples:2].set(source_of - shifted).at[2:2 + 2 * couples:2].set(sink + shifted)
    return lengths[jax.random.permutation(jax.random.fold_in(key, 2), number_of)]


def normal_values(rng, extent, width, limit, shards=(), kind=jnp.bfloat16):
    drawn = width * jax.random.normal(rng, extent, jnp.float32)
    if shards:
        drawn = drawn * levels(rng, extent, shards, -0.22, 0.18)
    return jnp.clip(drawn, -limit, limit).astype(kind)


def setup_inputs(seed: int = 0, part: int = 0) -> dict:
    keys = jax.random.split(jax.random.key(seed), 9)
    part_keys = jax.random.split(jax.random.fold_in(keys[8], part), 9)
    query_input = normal_values(part_keys[0], (TOKENS, W), 1.0, 6.0, ((0, 16),))
    key_input = normal_values(part_keys[1], (TOKENS, W), 1.0, 6.0, ((0, 16),))
    value_input = normal_values(part_keys[2], (TOKENS, W), 1.0, 6.0, ((0, 16),))
    output_grad = normal_values(part_keys[3], (TOKENS, W), 1.0, 6.0, ((0, 16),))
    short_taps = normal_values(keys[4], (3, SHORT_TAPS, W), SHORT_TAPS ** -0.5, 2.0, (), jnp.float32)
    long_filter = normal_values(keys[5], (TAPS, FILTERS), TAPS ** -0.5, 0.5)
    skip_gain = jnp.clip(1.0 + 0.18 * jax.random.normal(keys[6], (W,), jnp.float32), 0.1, 1.9)
    genome_ids = jnp.searchsorted(jnp.cumsum(ragged_sizes(part_keys[7], GENOMES, TOKENS, MOST_LEN, 2)), jnp.arange(TOKENS), side="right").astype(jnp.int32)
    return dict(query_input=query_input, key_input=key_input, value_input=value_input, output_grad=output_grad, short_taps=short_taps, long_filter=long_filter, skip_gain=skip_gain, genome_ids=genome_ids)


def short_forward(extended, weights, seg_source, seg_target):
    short_reach = weights.shape[0] - 1
    length = extended.shape[0] - short_reach
    result = jnp.zeros((length, extended.shape[1]), jnp.float32)
    for offset in range(short_reach + 1):
        first_row = short_reach - offset
        piece = extended[first_row:first_row + length].astype(jnp.float32)
        same_genome = (seg_source[first_row:first_row + length] == seg_target)[:, None]
        result = result + weights[offset][None, :] * jnp.where(same_genome, piece, jnp.zeros_like(piece))
    return result

def short_backward(extended, weights, seg_source, seg_target):
    short_reach = weights.shape[0] - 1
    length = extended.shape[0] - short_reach
    result = jnp.zeros((length, extended.shape[1]), jnp.float32)
    for offset in range(short_reach + 1):
        piece = extended[offset:offset + length].astype(jnp.float32)
        same_genome = (seg_source[offset:offset + length] == seg_target)[:, None]
        result = result + weights[offset][None, :] * jnp.where(same_genome, piece, jnp.zeros_like(piece))
    return result

def make_windows(extended, tap_count):
    length = extended.shape[0] - tap_count
    blocks = length // tap_count
    trailing = extended.shape[1:]
    return jnp.concatenate([extended[:length].reshape((blocks, tap_count) + trailing), extended[tap_count:].reshape((blocks, tap_count) + trailing)], axis=1)

def toeplitz_table(long_filter, forward):
    tap_count = long_filter.shape[0]
    target = jnp.arange(tap_count, dtype=jnp.int32)[:, None]
    source = jnp.arange(2 * tap_count, dtype=jnp.int32)[None, :]
    if forward:
        lag = tap_count + target - source
    else:
        lag = source - target
    valid = (lag >= 0) & (lag < tap_count)
    table = jnp.take(long_filter, jnp.clip(lag, 0, tap_count - 1).astype(jnp.int32), axis=0)
    return jnp.where(valid[:, :, None], table, jnp.zeros_like(table))

def grouped_conv(extended, seg_ext, long_filter, forward):
    tap_count, group_count = long_filter.shape
    length = extended.shape[0] - tap_count
    channels = extended.shape[1]
    blocks = length // tap_count
    windows = make_windows(extended, tap_count).reshape(blocks, 2 * tap_count, group_count, channels // group_count)
    seg_windows = make_windows(seg_ext, tap_count)
    if forward:
        seg_targets = seg_ext[tap_count:].reshape(blocks, tap_count)
    else:
        seg_targets = seg_ext[:length].reshape(blocks, tap_count)
    table = toeplitz_table(long_filter.astype(jnp.float32), forward)

    def one_block(inputs):
        block_rows, seg_source, seg_target = inputs
        same_genome = (seg_target[:, None] == seg_source[None, :]).astype(jnp.float32)
        masked = table * same_genome[:, :, None]
        return jnp.einsum('tsg,sgc->tgc', masked, block_rows.astype(jnp.float32), precision=lax.Precision.HIGHEST)
    return lax.map(one_block, (windows, seg_windows, seg_targets)).reshape(length, channels)

def filter_terms(conv_grad, extended, seg_ext, tap_count, group_count):
    length = conv_grad.shape[0]
    channels = conv_grad.shape[1]
    blocks = length // tap_count
    values = make_windows(extended, tap_count).reshape(blocks, 2 * tap_count, group_count, channels // group_count)
    grads = conv_grad.reshape(blocks, tap_count, group_count, channels // group_count)
    seg_windows = make_windows(seg_ext, tap_count)
    seg_targets = seg_ext[tap_count:].reshape(blocks, tap_count)

    def one_block(inputs):
        grad_rows, value_rows, seg_source, seg_target = inputs
        same_genome = (seg_target[:, None] == seg_source[None, :]).astype(jnp.float32)
        products = jnp.einsum('tgc,sgc->tsg', grad_rows.astype(jnp.float32), value_rows.astype(jnp.float32), precision=lax.Precision.HIGHEST) * same_genome[:, :, None]
        flat = products.reshape(tap_count * 2 * tap_count, group_count)
        flat = jnp.concatenate([flat, jnp.zeros((tap_count, group_count), jnp.float32)], axis=0)
        diagonal = flat.reshape(tap_count, 2 * tap_count + 1, group_count)[:, 1:tap_count + 1, :]
        return lax.optimization_barrier(jnp.sum(diagonal, axis=0))[::-1]
    return lax.optimization_barrier(jnp.sum(lax.map(one_block, (grads, values, seg_windows, seg_targets)), axis=0))

def reference(query_input, key_input, value_input, output_grad, short_taps, long_filter, skip_gain, genome_ids):
    tap_count, group_count = long_filter.shape
    short_reach = short_taps.shape[1] - 1
    length = query_input.shape[0]
    channels = query_input.shape[1]
    seg_pad = jnp.pad(genome_ids, (tap_count, tap_count), constant_values=-1)
    seg_front = seg_pad[:length + tap_count]
    seg_back = seg_pad[tap_count:]
    short_source = seg_front[tap_count - short_reach:]
    back_source = seg_back[:length + short_reach]
    short_zeros = jnp.zeros((short_reach, channels), jnp.bfloat16)
    long_zeros = jnp.zeros((tap_count, channels), jnp.bfloat16)
    query_short = short_forward(jnp.concatenate([short_zeros, query_input], 0), short_taps[0], short_source, genome_ids)
    key_short = short_forward(jnp.concatenate([short_zeros, key_input], 0), short_taps[1], short_source, genome_ids)
    value_short = short_forward(jnp.concatenate([short_zeros, value_input], 0), short_taps[2], short_source, genome_ids)
    gated_pair = (key_short * value_short).astype(jnp.bfloat16)
    extended = jnp.concatenate([long_zeros, gated_pair], 0)
    conv_out = grouped_conv(extended, seg_front, long_filter, True) + skip_gain[None, :] * gated_pair.astype(jnp.float32)
    section_out = (query_short * conv_out).astype(jnp.bfloat16)
    cotangent = output_grad.astype(jnp.float32)
    conv_grad = (cotangent * query_short).astype(jnp.bfloat16)
    query_grad_short = (cotangent * conv_out).astype(jnp.bfloat16)
    grad_ext = jnp.concatenate([conv_grad, long_zeros], 0)
    pair_grad = grouped_conv(grad_ext, seg_back, long_filter, False) + skip_gain[None, :] * conv_grad.astype(jnp.float32)
    key_grad_short = (pair_grad * value_short).astype(jnp.bfloat16)
    value_grad_short = (pair_grad * key_short).astype(jnp.bfloat16)
    grad_query = short_backward(jnp.concatenate([query_grad_short, short_zeros], 0), short_taps[0], back_source, genome_ids).astype(jnp.bfloat16)
    grad_key = short_backward(jnp.concatenate([key_grad_short, short_zeros], 0), short_taps[1], back_source, genome_ids).astype(jnp.bfloat16)
    grad_value = short_backward(jnp.concatenate([value_grad_short, short_zeros], 0), short_taps[2], back_source, genome_ids).astype(jnp.bfloat16)
    partial_terms = filter_terms(conv_grad, extended, seg_front, tap_count, group_count)
    filter_grad = partial_terms * (1.0 / math.sqrt(GROUP_SIZE * TOKENS))
    return (section_out, grad_query, grad_key, grad_value, filter_grad)
```

```python
import functools
import math

import jax
import jax.numpy as jnp
from jax import lax
from jax.experimental import pallas as pl
from jax.experimental.pallas import tpu as pltpu
from jax.sharding import PartitionSpec as P

MESH = pl.DeviceIdType.MESH
LANES = 128
RB = 16
PAD = 16


def lanes_of(index):
    return pl.ds(pl.multiple_of(index * LANES, LANES), LANES)


def kernel(
    n, chunks, width,
    q_ref, k_ref, v_ref, d_ref, taps_ref, base_ref, gain_ref, mshort_ref, mf_ref, mb_ref, lm_ref,
    so_ref, gq_ref, gk_ref, gv_ref, f_ref,
    rim_q, rim_k, rim_v, xf, xb, qs, ks, vs, hf, hb, eq, ek, ev, scr,
    rim_ss, rim_rs, gp_ss, gp_rs, cg_ss, cg_rs, eb_ss, eb_rs,
):
    rows, channels = q_ref.shape
    short = taps_ref.shape[1]
    groups = LANES // width
    steps = channels // LANES // chunks
    me = lax.axis_index("seq")
    grp = lax.axis_index("grp")
    has_left = me > 0
    has_right = me < n - 1
    left = (grp, lax.max(me - 1, 0))
    right = (grp, lax.min(me + 1, n - 1))
    f32, bf16 = jnp.float32, jnp.bfloat16
    barrier = pltpu.get_barrier_semaphore()

    @pl.when(has_left)
    def _():
        pl.semaphore_signal(barrier, inc=1, device_id=left, device_id_type=MESH)

    @pl.when(has_right)
    def _():
        pl.semaphore_signal(barrier, inc=1, device_id=right, device_id_type=MESH)

    pl.semaphore_wait(barrier, jnp.where(has_left, 1, 0) + jnp.where(has_right, 1, 0))

    def remote(src, dst, ssem, rsem, where):
        return pltpu.make_async_remote_copy(
            src_ref=src, dst_ref=dst, send_sem=ssem, recv_sem=rsem, device_id=where, device_id_type=MESH
        )

    rim_copies = [
        remote(src.at[pl.ds(rows - PAD, PAD), :], dst, rim_ss.at[i], rim_rs.at[i], right)
        for i, (src, dst) in enumerate(((q_ref, rim_q), (k_ref, rim_k), (v_ref, rim_v)))
    ]

    @pl.when(has_right)
    def _():
        for copy in rim_copies:
            copy.start()

    taps = rows
    window = 2 * taps
    rest = xf.shape[0] - 2 * rows
    xf[pl.ds(2 * rows, rest), :] = jnp.zeros((rest, channels), bf16)
    xb[pl.ds(2 * rows, rest), :] = jnp.zeros((rest, channels), bf16)

    def build(i, carry):
        for which, dest in ((0, hf), (1, hb)):
            tile = base_ref[which, pl.ds(pl.multiple_of(i * groups, groups), groups), :]
            for g in range(groups):
                row = jnp.broadcast_to(tile[g : g + 1, :], (RB, window))
                skew = pltpu.roll(row, 0, 1, stride=1, stride_axis=0)
                dest[pl.ds(pl.multiple_of((i * groups + g) * RB, RB), RB), :] = skew.astype(bf16)
        return carry

    lax.fori_loop(0, channels // LANES, build, 0)

    @pl.when(has_left)
    def _():
        for copy in rim_copies:
            copy.wait_recv()

    @pl.when(jnp.logical_not(has_left))
    def _():
        for rim in (rim_q, rim_k, rim_v):
            rim[...] = jnp.zeros_like(rim)
        xf[pl.ds(0, rows), :] = jnp.zeros((rows, channels), bf16)

    @pl.when(jnp.logical_not(has_right))
    def _():
        xb[pl.ds(rows, rows), :] = jnp.zeros((rows, channels), bf16)
        for rim in (eq, ek, ev):
            rim[pl.ds(rows, PAD), :] = jnp.zeros((PAD, channels), bf16)

    def forward(slot, x_ref, rim, col):
        scr[slot, 0:PAD, :] = rim[:, col].astype(f32)
        scr[slot, PAD : PAD + rows, :] = x_ref[:, col].astype(f32)
        total = taps_ref[slot, 0:1, col] * scr[slot, PAD : PAD + rows, :]
        for j in range(1, short):
            total = total + taps_ref[slot, j : j + 1, col] * (
                mshort_ref[j - 1] * scr[slot, PAD - j : PAD - j + rows, :]
            )
        return total

    def first(i, carry):
        col = lanes_of(i)
        query = forward(0, q_ref, rim_q, col)
        qs[:, col] = query
        xb[0:rows, col] = (d_ref[:, col].astype(f32) * query).astype(bf16)
        key = forward(1, k_ref, rim_k, col)
        ks[:, col] = key
        value = forward(2, v_ref, rim_v, col)
        vs[:, col] = value
        xf[rows : 2 * rows, col] = (key * value).astype(bf16)
        return carry

    gp_copies, cg_copies, eb_copies = [], [], []
    for chunk in range(chunks):
        lo = chunk * steps * LANES
        span = pl.ds(lo, steps * LANES)
        gp_copies.append(remote(
            xf.at[pl.ds(rows, rows), span], xf.at[pl.ds(0, rows), span], gp_ss.at[chunk], gp_rs.at[chunk], right))
        cg_copies.append(remote(
            xb.at[pl.ds(0, rows), span], xb.at[pl.ds(rows, rows), span], cg_ss.at[chunk], cg_rs.at[chunk], left))
        eb_copies.append([
            remote(e.at[pl.ds(0, PAD), span], e.at[pl.ds(rows, PAD), span],
                   eb_ss.at[chunk * 3 + i], eb_rs.at[chunk * 3 + i], left)
            for i, e in enumerate((eq, ek, ev))
        ])

    for chunk in range(chunks):
        lax.fori_loop(chunk * steps, (chunk + 1) * steps, first, 0)

        @pl.when(has_right)
        def _():
            gp_copies[chunk].start()

        @pl.when(has_left)
        def _():
            cg_copies[chunk].start()

    lane_group = lax.broadcasted_iota(jnp.int32, (RB, LANES), 1) // width

    def diagonal(out):
        y = out[0:RB]
        for g in range(1, groups):
            y = jnp.where(lane_group == g, out[g * RB : (g + 1) * RB], y)
        return y

    def second(i, carry):
        col = lanes_of(i)
        hrows = pl.ds(pl.multiple_of(i * groups * RB, groups * RB), groups * RB)
        gain = gain_ref[0:1, col]
        total = None
        for a in range(rows // RB):
            own = slice(a * RB, (a + 1) * RB)
            mf = mf_ref[own, :]
            source = xf[a * RB : a * RB + window, col]
            grads = xb[a * RB : a * RB + window, col]
            table = (hf[hrows, :].reshape(groups, RB, window) * mf[None]).reshape(groups * RB, window)
            conv = diagonal(jnp.dot(table, source, preferred_element_type=f32))
            pair = xf[rows + a * RB : rows + (a + 1) * RB, col]
            conv = conv + gain * pair.astype(f32)
            so_ref[own, col] = (qs[own, col] * conv).astype(bf16)
            eq[own, col] = (d_ref[own, col].astype(f32) * conv).astype(bf16)
            table = (hb[hrows, :].reshape(groups, RB, window) * mb_ref[own, :][None]).reshape(groups * RB, window)
            back = diagonal(jnp.dot(table, grads, preferred_element_type=f32))
            grad = xb[own, col]
            back = back + gain * grad.astype(f32)
            ek[own, col] = (back * vs[own, col]).astype(bf16)
            ev[own, col] = (back * ks[own, col]).astype(bf16)
            spread = (grad[None] * lm_ref[...]).reshape(groups * RB, LANES)
            terms = lax.dot_general(spread, source, (((1,), (1,)), ((), ())), preferred_element_type=f32)
            terms = terms.reshape(groups, RB, window) * mf.astype(f32)[None]
            total = terms if total is None else total + terms
        half = RB // 2
        upper = total[:, half:].reshape(groups * half, window)
        total = total[:, :half].reshape(groups * half, window) + pltpu.roll(upper, window - half, 1)
        sub = lax.broadcasted_iota(jnp.int32, (groups * half, window), 0)
        shift = 1
        while shift < half:
            total = jnp.where((sub & shift) != 0, pltpu.roll(total, window - shift, 1), total)
            shift *= 2
        terms = jnp.sum(total.reshape(groups, half, window), axis=1)
        terms = pltpu.roll(terms, window - 1, 1)
        f_ref[pl.ds(pl.multiple_of(i * groups, groups), groups), :] = terms[:, :taps]
        return carry

    for chunk in range(chunks):
        @pl.when(has_left)
        def _():
            gp_copies[chunk].wait_recv()

        @pl.when(has_right)
        def _():
            cg_copies[chunk].wait_recv()

        lax.fori_loop(chunk * steps, (chunk + 1) * steps, second, 0)

        @pl.when(has_left)
        def _():
            for copy in eb_copies[chunk]:
                copy.start()

    def backward(slot, e_ref, out_ref, col):
        scr[slot] = e_ref[:, col].astype(f32)
        total = taps_ref[slot, 0:1, col] * scr[slot, 0:rows, :]
        for j in range(1, short):
            total = total + taps_ref[slot, j : j + 1, col] * (
                mshort_ref[short - 2 + j] * scr[slot, j : j + rows, :]
            )
        out_ref[:, col] = total.astype(bf16)

    def third(i, carry):
        col = lanes_of(i)
        backward(0, eq, gq_ref, col)
        backward(1, ek, gk_ref, col)
        backward(2, ev, gv_ref, col)
        return carry

    for chunk in range(chunks):
        @pl.when(has_right)
        def _():
            for copy in eb_copies[chunk]:
                copy.wait_recv()

        lax.fori_loop(chunk * steps, (chunk + 1) * steps, third, 0)

    @pl.when(has_right)
    def _():
        for copy in rim_copies:
            copy.wait_send()
        for copy in gp_copies:
            copy.wait_send()

    @pl.when(has_left)
    def _():
        for copy in cg_copies:
            copy.wait_send()
        for copies in eb_copies:
            for copy in copies:
                copy.wait_send()


def body(q, k, v, d, short_taps, long_filter, skip_gain, genome_ids):
    rows, channels = q.shape
    taps, filters = long_filter.shape
    width = channels // filters
    groups = LANES // width
    short = short_taps.shape[1]
    n = lax.axis_size("seq")
    me = lax.axis_index("seq")
    f32, bf16 = jnp.float32, jnp.bfloat16
    window = 2 * taps
    chunks = 4
    ext = 2 * rows + window - RB - rows
    ext = max(ext, 3 * rows - RB)

    padded = jnp.pad(genome_ids, (taps, 2 * taps), constant_values=-1)
    ids = lax.dynamic_slice_in_dim(padded, me * rows, 2 * taps + 2 * rows, 0)
    own = ids[taps : taps + rows]
    blocks = rows // RB
    front = jnp.stack([ids[a * RB : a * RB + window] for a in range(blocks)])
    back = jnp.stack([ids[taps + a * RB : taps + a * RB + window] for a in range(blocks)])
    own_blocks = own.reshape(blocks, RB, 1)
    mf = (own_blocks == front[:, None, :]).astype(bf16).reshape(rows, window)
    mb = (own_blocks == back[:, None, :]).astype(bf16).reshape(rows, window)
    mshort = jnp.stack(
        [own == ids[taps - j : taps - j + rows] for j in range(1, short)]
        + [own == ids[taps + j : taps + j + rows] for j in range(1, short)]
    ).astype(f32)
    mshort = jnp.broadcast_to(mshort[:, :, None], (2 * (short - 1), rows, LANES))
    filt = long_filter.astype(f32).T
    base = jnp.stack([
        jnp.pad(filt[:, ::-1], ((0, 0), (1, window - taps - 1))),
        jnp.pad(filt, ((0, 0), (0, window - taps))),
    ])
    lane = lax.broadcasted_iota(jnp.int32, (groups, RB, LANES), 2) // width
    lm = (lane == lax.broadcasted_iota(jnp.int32, (groups, RB, LANES), 0)).astype(bf16)

    big = jax.ShapeDtypeStruct((rows, channels), bf16)
    vm = pl.BlockSpec(memory_space=pltpu.VMEM)
    dma = pltpu.SemaphoreType.DMA
    so, gq, gk, gv, terms = pl.pallas_call(
        functools.partial(kernel, n, chunks, width),
        out_shape=(big, big, big, big, jax.ShapeDtypeStruct((filters, taps), f32)),
        in_specs=[vm] * 11,
        out_specs=(vm,) * 5,
        scratch_shapes=[
            pltpu.VMEM((PAD, channels), bf16),
            pltpu.VMEM((PAD, channels), bf16),
            pltpu.VMEM((PAD, channels), bf16),
            pltpu.VMEM((ext, channels), bf16),
            pltpu.VMEM((ext, channels), bf16),
            pltpu.VMEM((rows, channels), f32),
            pltpu.VMEM((rows, channels), f32),
            pltpu.VMEM((rows, channels), f32),
            pltpu.VMEM((filters * RB, window), bf16),
            pltpu.VMEM((filters * RB, window), bf16),
            pltpu.VMEM((rows + PAD, channels), bf16),
            pltpu.VMEM((rows + PAD, channels), bf16),
            pltpu.VMEM((rows + PAD, channels), bf16),
            pltpu.VMEM((3, rows + PAD, LANES), f32),
            dma((3,)), dma((3,)),
            dma((chunks,)), dma((chunks,)),
            dma((chunks,)), dma((chunks,)),
            dma((3 * chunks,)), dma((3 * chunks,)),
        ],
        compiler_params=pltpu.CompilerParams(
            collective_id=0, has_side_effects=True, vmem_limit_bytes=56 * 1024 * 1024
        ),
    )(q, k, v, d, short_taps, base, skip_gain.reshape(1, channels), mshort, mf, mb, lm)
    scale = 1.0 / math.sqrt(width * rows * n)
    summed = lax.psum(terms, "seq")
    return so, gq, gk, gv, summed[:, ::-1].T * scale


def solution(mesh):
    tile = P(("grp", "seq"), None)
    return jax.shard_map(
        body,
        mesh=mesh,
        in_specs=(tile, tile, tile, tile, P(), P(), P(), P("grp")),
        out_specs=(tile, tile, tile, tile, P("grp", None)),
        check_vma=False,
    )
```

```python
import functools
import math

import jax
import jax.numpy as jnp
from jax import lax
from jax.experimental import pallas as pl
from jax.experimental.pallas import tpu as pltpu
from jax.sharding import PartitionSpec as P

MESH = pl.DeviceIdType.MESH
LANES = 128
RB = 16
PAD = 16
DEPTH = 3


def lanes_of(index):
    return pl.ds(pl.multiple_of(index * LANES, LANES), LANES)


def kernel(
    n, chunks, width, scale,
    q_ref, k_ref, v_ref, d_ref, taps_ref, base_ref, gain_ref, mshort_ref, mf_ref, mb_ref, lm_ref, mt_ref,
    so_ref, gq_ref, gk_ref, gv_ref, f_ref,
    rim_q, rim_k, rim_v, xf, xb, qs, ks, vs, hf, hb, eq, ek, ev, scr,
    parts, inbox, done, rim_ss, rim_rs, gp_ss, gp_rs, cg_ss, cg_rs, eb_ss, eb_rs, ps_ss, ps_rs, bc_ss, bc_rs,
):
    rows, channels = q_ref.shape
    short = taps_ref.shape[1]
    groups = LANES // width
    steps = channels // LANES // chunks
    me = lax.axis_index("seq")
    grp = lax.axis_index("grp")
    has_left = me > 0
    has_right = me < n - 1
    left = (grp, lax.max(me - 1, 0))
    right = (grp, lax.min(me + 1, n - 1))
    f32, bf16 = jnp.float32, jnp.bfloat16
    barrier = pltpu.get_barrier_semaphore()

    def peer_of(offset):
        return lax.rem(me + offset, n)

    def greet(offset, carry):
        pl.semaphore_signal(barrier, inc=1, device_id=(grp, peer_of(offset)), device_id_type=MESH)
        return carry

    lax.fori_loop(1, n, greet, 0)
    pl.semaphore_wait(barrier, n - 1)

    def remote(src, dst, ssem, rsem, where):
        return pltpu.make_async_remote_copy(
            src_ref=src, dst_ref=dst, send_sem=ssem, recv_sem=rsem, device_id=where, device_id_type=MESH
        )

    rim_copies = [
        remote(src.at[pl.ds(rows - PAD, PAD), :], dst, rim_ss.at[i], rim_rs.at[i], right)
        for i, (src, dst) in enumerate(((q_ref, rim_q), (k_ref, rim_k), (v_ref, rim_v)))
    ]

    @pl.when(has_right)
    def _():
        for copy in rim_copies:
            copy.start()

    taps = rows
    window = 2 * taps
    reach = taps + RB
    rest = xf.shape[0] - 2 * rows
    xf[pl.ds(2 * rows, rest), :] = jnp.zeros((rest, channels), bf16)
    xb[pl.ds(2 * rows, rest), :] = jnp.zeros((rest, channels), bf16)

    def build(i, carry):
        for which, dest in ((0, hf), (1, hb)):
            tile = base_ref[which, pl.ds(pl.multiple_of(i * groups, groups), groups), :]
            for g in range(groups):
                row = jnp.broadcast_to(tile[g : g + 1, :], (RB, window))
                skew = pltpu.roll(row, 0, 1, stride=1, stride_axis=0)
                dest[pl.ds(pl.multiple_of((i * groups + g) * RB, RB), RB), :] = skew.astype(bf16)
        return carry

    lax.fori_loop(0, channels // LANES, build, 0)

    @pl.when(has_left)
    def _():
        for copy in rim_copies:
            copy.wait_recv()

    @pl.when(jnp.logical_not(has_left))
    def _():
        for rim in (rim_q, rim_k, rim_v):
            rim[...] = jnp.zeros_like(rim)
        xf[pl.ds(0, rows), :] = jnp.zeros((rows, channels), bf16)

    @pl.when(jnp.logical_not(has_right))
    def _():
        xb[pl.ds(rows, rows), :] = jnp.zeros((rows, channels), bf16)
        for rim in (eq, ek, ev):
            rim[pl.ds(rows, PAD), :] = jnp.zeros((PAD, channels), bf16)

    def forward(slot, x_ref, rim, col):
        scr[slot, 0:PAD, :] = rim[:, col].astype(f32)
        scr[slot, PAD : PAD + rows, :] = x_ref[:, col].astype(f32)
        total = taps_ref[slot, 0:1, col] * scr[slot, PAD : PAD + rows, :]
        for j in range(1, short):
            total = total + taps_ref[slot, j : j + 1, col] * (
                mshort_ref[j - 1] * scr[slot, PAD - j : PAD - j + rows, :]
            )
        return total

    def first(i, carry):
        col = lanes_of(i)
        query = forward(0, q_ref, rim_q, col)
        qs[:, col] = query
        xb[0:rows, col] = (d_ref[:, col].astype(f32) * query).astype(bf16)
        key = forward(1, k_ref, rim_k, col)
        ks[:, col] = key
        value = forward(2, v_ref, rim_v, col)
        vs[:, col] = value
        xf[rows : 2 * rows, col] = (key * value).astype(bf16)
        return carry

    gp_copies, cg_copies, eb_copies = [], [], []
    for chunk in range(chunks):
        lo = chunk * steps * LANES
        span = pl.ds(lo, steps * LANES)
        gp_copies.append(remote(
            xf.at[pl.ds(rows, rows), span], xf.at[pl.ds(0, rows), span], gp_ss.at[chunk], gp_rs.at[chunk], right))
        cg_copies.append(remote(
            xb.at[pl.ds(0, rows), span], xb.at[pl.ds(rows, rows), span], cg_ss.at[chunk], cg_rs.at[chunk], left))
        eb_copies.append([
            remote(e.at[pl.ds(0, PAD), span], e.at[pl.ds(rows, PAD), span],
                   eb_ss.at[chunk * 3 + i], eb_rs.at[chunk * 3 + i], left)
            for i, e in enumerate((eq, ek, ev))
        ])

    for chunk in range(chunks):
        lax.fori_loop(chunk * steps, (chunk + 1) * steps, first, 0)

        if chunk < DEPTH:
            @pl.when(has_right)
            def _():
                gp_copies[chunk].start()

            @pl.when(has_left)
            def _():
                cg_copies[chunk].start()

    lane_group = lax.broadcasted_iota(jnp.int32, (RB, LANES), 1) // width

    def diagonal(out):
        y = out[0:RB]
        for g in range(1, groups):
            y = jnp.where(lane_group == g, out[g * RB : (g + 1) * RB], y)
        return y

    def part_copy(owner, sender):
        return remote(parts.at[owner], inbox.at[sender], ps_ss.at[owner], ps_rs.at[sender], (grp, owner))

    def done_copy(owner, peer):
        return remote(done.at[owner], done.at[owner], bc_ss.at[peer], bc_rs.at[owner], (grp, peer))

    def over_peers(act):
        def step(offset, carry):
            act(peer_of(offset))
            return carry

        lax.fori_loop(1, n, step, 0)

    per = parts.shape[1]

    def second(i, carry):
        col = lanes_of(i)
        hrows = pl.ds(pl.multiple_of(i * groups * RB, groups * RB), groups * RB)
        gain = gain_ref[0:1, col]
        total = None
        for a in range(rows // RB):
            own = slice(a * RB, (a + 1) * RB)
            mf = mf_ref[own, :]
            source = xf[a * RB : a * RB + window, col]
            grads = xb[a * RB : a * RB + window, col]
            table = (hf[hrows, :].reshape(groups, RB, window) * mf[None]).reshape(groups * RB, window)
            conv = diagonal(jnp.dot(table, source, preferred_element_type=f32))
            pair = xf[rows + a * RB : rows + (a + 1) * RB, col]
            conv = conv + gain * pair.astype(f32)
            so_ref[own, col] = (qs[own, col] * conv).astype(bf16)
            eq[own, col] = (d_ref[own, col].astype(f32) * conv).astype(bf16)
            table = (hb[hrows, :].reshape(groups, RB, window) * mb_ref[own, :][None]).reshape(groups * RB, window)
            back = diagonal(jnp.dot(table, grads, preferred_element_type=f32))
            grad = xb[own, col]
            back = back + gain * grad.astype(f32)
            ek[own, col] = (back * vs[own, col]).astype(bf16)
            ev[own, col] = (back * ks[own, col]).astype(bf16)
            spread = (grad[None] * lm_ref[...]).reshape(groups * RB, LANES)
            terms = lax.dot_general(
                xf[a * RB : a * RB + reach, col], spread, (((1,), (1,)), ((), ())), preferred_element_type=f32)
            terms = terms * mt_ref[a]
            total = terms if total is None else total + terms
        total = jnp.concatenate([total, jnp.zeros((window - reach, groups * RB), f32)], axis=0)
        total = total.T.reshape(groups, RB, window)
        half = RB // 2
        upper = total[:, half:].reshape(groups * half, window)
        total = total[:, :half].reshape(groups * half, window) + pltpu.roll(upper, window - half, 1)
        sub = lax.broadcasted_iota(jnp.int32, (groups * half, window), 0)
        shift = 1
        while shift < half:
            total = jnp.where((sub & shift) != 0, pltpu.roll(total, window - shift, 1), total)
            shift *= 2
        terms = jnp.sum(total.reshape(groups, half, window), axis=1)
        terms = pltpu.roll(terms, window - 1, 1)
        if per >= groups:
            parts[i * groups // per, pl.ds(pl.multiple_of(i * groups % per, groups), groups), :] = terms[:, :taps]
        else:
            for m in range(groups // per):
                parts[i * (groups // per) + m] = terms[m * per : (m + 1) * per, :taps]
        return carry

    for chunk in range(chunks):
        @pl.when(has_left)
        def _():
            gp_copies[chunk].wait_recv()

        @pl.when(has_right)
        def _():
            cg_copies[chunk].wait_recv()

        if chunk + DEPTH < chunks:
            @pl.when(has_right)
            def _():
                gp_copies[chunk].wait_send()
                gp_copies[chunk + DEPTH].start()

            @pl.when(has_left)
            def _():
                cg_copies[chunk].wait_send()
                cg_copies[chunk + DEPTH].start()

        lax.fori_loop(chunk * steps, (chunk + 1) * steps, second, 0)

        @pl.when(has_left)
        def _():
            for copy in eb_copies[chunk]:
                copy.start()

    over_peers(lambda peer: part_copy(peer, me).start())

    def backward(slot, e_ref, out_ref, col):
        scr[slot] = e_ref[:, col].astype(f32)
        total = taps_ref[slot, 0:1, col] * scr[slot, 0:rows, :]
        for j in range(1, short):
            total = total + taps_ref[slot, j : j + 1, col] * (
                mshort_ref[short - 2 + j] * scr[slot, j : j + rows, :]
            )
        out_ref[:, col] = total.astype(bf16)

    def third(i, carry):
        col = lanes_of(i)
        backward(0, eq, gq_ref, col)
        backward(1, ek, gk_ref, col)
        backward(2, ev, gv_ref, col)
        return carry

    for chunk in range(chunks):
        @pl.when(has_right)
        def _():
            for copy in eb_copies[chunk]:
                copy.wait_recv()

        lax.fori_loop(chunk * steps, (chunk + 1) * steps, third, 0)
        if chunk == chunks // 2 - 1:
            over_peers(lambda peer: part_copy(peer, peer).wait_recv())
            total = parts[me]

            def add(offset, total):
                return total + inbox[peer_of(offset)]

            done[me] = lax.fori_loop(1, n, add, total)
            over_peers(lambda peer: done_copy(me, peer).start())

    @pl.when(has_right)
    def _():
        for copy in rim_copies:
            copy.wait_send()
        for copy in gp_copies[chunks - DEPTH :]:
            copy.wait_send()

    @pl.when(has_left)
    def _():
        for copy in cg_copies[chunks - DEPTH :]:
            copy.wait_send()
        for copies in eb_copies:
            for copy in copies:
                copy.wait_send()

    over_peers(lambda peer: part_copy(peer, peer).wait_send())
    over_peers(lambda peer: done_copy(peer, peer).wait_recv())
    over_peers(lambda peer: done_copy(me, peer).wait_send())
    flip = (
        lax.broadcasted_iota(jnp.int32, (taps, taps), 0) + lax.broadcasted_iota(jnp.int32, (taps, taps), 1)
        == taps - 1
    ).astype(f32)
    f_ref[...] = scale * lax.dot_general(
        flip, done[...].reshape(n * per, taps), (((1,), (1,)), ((), ())),
        precision=lax.Precision.HIGHEST, preferred_element_type=f32)


def body(q, k, v, d, short_taps, long_filter, skip_gain, genome_ids):
    rows, channels = q.shape
    taps, filters = long_filter.shape
    width = channels // filters
    groups = LANES // width
    short = short_taps.shape[1]
    n = lax.axis_size("seq")
    me = lax.axis_index("seq")
    f32, bf16 = jnp.float32, jnp.bfloat16
    window = 2 * taps
    chunks = 8
    ext = 2 * rows + window - RB - rows
    ext = max(ext, 3 * rows - RB)

    padded = jnp.pad(genome_ids, (taps, 2 * taps), constant_values=-1)
    ids = lax.dynamic_slice_in_dim(padded, me * rows, 2 * taps + 2 * rows, 0)
    own = ids[taps : taps + rows]
    blocks = rows // RB
    front = jnp.stack([ids[a * RB : a * RB + window] for a in range(blocks)])
    back = jnp.stack([ids[taps + a * RB : taps + a * RB + window] for a in range(blocks)])
    own_blocks = own.reshape(blocks, RB, 1)
    mf = (own_blocks == front[:, None, :]).astype(bf16).reshape(rows, window)
    mb = (own_blocks == back[:, None, :]).astype(bf16).reshape(rows, window)
    same_t = (own.reshape(blocks, 1, RB) == front[:, : taps + RB, None]).astype(f32)
    mt = jnp.tile(same_t, (1, 1, groups))
    mshort = jnp.stack(
        [own == ids[taps - j : taps - j + rows] for j in range(1, short)]
        + [own == ids[taps + j : taps + j + rows] for j in range(1, short)]
    ).astype(f32)
    mshort = jnp.broadcast_to(mshort[:, :, None], (2 * (short - 1), rows, LANES))
    filt = long_filter.astype(f32).T
    base = jnp.stack([
        jnp.pad(filt[:, ::-1], ((0, 0), (1, window - taps - 1))),
        jnp.pad(filt, ((0, 0), (0, window - taps))),
    ])
    lane = lax.broadcasted_iota(jnp.int32, (groups, RB, LANES), 2) // width
    lm = (lane == lax.broadcasted_iota(jnp.int32, (groups, RB, LANES), 0)).astype(bf16)

    scale = 1.0 / math.sqrt(width * rows * n)
    big = jax.ShapeDtypeStruct((rows, channels), bf16)
    vm = pl.BlockSpec(memory_space=pltpu.VMEM)
    dma = pltpu.SemaphoreType.DMA
    so, gq, gk, gv, terms = pl.pallas_call(
        functools.partial(kernel, n, chunks, width, scale),
        out_shape=(big, big, big, big, jax.ShapeDtypeStruct((taps, filters), f32)),
        in_specs=[vm] * 12,
        out_specs=(vm,) * 5,
        scratch_shapes=[
            pltpu.VMEM((PAD, channels), bf16),
            pltpu.VMEM((PAD, channels), bf16),
            pltpu.VMEM((PAD, channels), bf16),
            pltpu.VMEM((ext, channels), bf16),
            pltpu.VMEM((ext, channels), bf16),
            pltpu.VMEM((rows, channels), f32),
            pltpu.VMEM((rows, channels), f32),
            pltpu.VMEM((rows, channels), f32),
            pltpu.VMEM((filters * RB, window), bf16),
            pltpu.VMEM((filters * RB, window), bf16),
            pltpu.VMEM((rows + PAD, channels), bf16),
            pltpu.VMEM((rows + PAD, channels), bf16),
            pltpu.VMEM((rows + PAD, channels), bf16),
            pltpu.VMEM((3, rows + PAD, LANES), f32),
            pltpu.VMEM((n, filters // n, taps), f32),
            pltpu.VMEM((n, filters // n, taps), f32),
            pltpu.VMEM((n, filters // n, taps), f32),
            dma((3,)), dma((3,)),
            dma((chunks,)), dma((chunks,)),
            dma((chunks,)), dma((chunks,)),
            dma((3 * chunks,)), dma((3 * chunks,)),
            dma((n,)), dma((n,)), dma((n,)), dma((n,)),
        ],
        compiler_params=pltpu.CompilerParams(
            collective_id=0, has_side_effects=True, vmem_limit_bytes=56 * 1024 * 1024
        ),
    )(q, k, v, d, short_taps, base, skip_gain.reshape(1, channels), mshort, mf, mb, lm, mt)
    return so, gq, gk, gv, terms


def solution(mesh):
    tile = P(("grp", "seq"), None)
    return jax.shard_map(
        body,
        mesh=mesh,
        in_specs=(tile, tile, tile, tile, P(), P(), P(), P("grp")),
        out_specs=(tile, tile, tile, tile, P("grp", None)),
        check_vma=False,
    )
```

```python
import functools
import math

import jax
import jax.numpy as jnp
from jax import lax
from jax.experimental import pallas as pl
from jax.experimental.pallas import tpu as pltpu
from jax.sharding import PartitionSpec as P

MESH = pl.DeviceIdType.MESH
LANES = 128
RB = 16
PAD = 16
DEPTH = 3


def lanes_of(index):
    return pl.ds(pl.multiple_of(index * LANES, LANES), LANES)


def kernel(
    n, chunks, width, scale,
    q_ref, k_ref, v_ref, d_ref, taps_ref, base_ref, gain_ref, mshort_ref, mf_ref, mb_ref, lm_ref, mt_ref,
    so_ref, gq_ref, gk_ref, gv_ref, f_ref,
    rim_q, rim_k, rim_v, xf, xb, qs, ks, vs, hf, hb, eq, ek, ev, scr,
    parts, inbox, done, rim_ss, rim_rs, gp_ss, gp_rs, cg_ss, cg_rs, eb_ss, eb_rs, ps_ss, ps_rs, bc_ss, bc_rs,
):
    rows, channels = q_ref.shape
    short = taps_ref.shape[1]
    groups = LANES // width
    steps = channels // LANES // chunks
    me = lax.axis_index("seq")
    grp = lax.axis_index("grp")
    has_left = me > 0
    has_right = me < n - 1
    left = (grp, lax.max(me - 1, 0))
    right = (grp, lax.min(me + 1, n - 1))
    f32, bf16 = jnp.float32, jnp.bfloat16
    barrier = pltpu.get_barrier_semaphore()

    def peer_of(offset):
        return lax.rem(me + offset, n)

    def greet(offset, carry):
        pl.semaphore_signal(barrier, inc=1, device_id=(grp, peer_of(offset)), device_id_type=MESH)
        return carry

    lax.fori_loop(1, n, greet, 0)
    pl.semaphore_wait(barrier, n - 1)

    def remote(src, dst, ssem, rsem, where):
        return pltpu.make_async_remote_copy(
            src_ref=src, dst_ref=dst, send_sem=ssem, recv_sem=rsem, device_id=where, device_id_type=MESH
        )

    rim_copies = [
        remote(src.at[pl.ds(rows - PAD, PAD), :], dst, rim_ss.at[i], rim_rs.at[i], right)
        for i, (src, dst) in enumerate(((q_ref, rim_q), (k_ref, rim_k), (v_ref, rim_v)))
    ]

    @pl.when(has_right)
    def _():
        for copy in rim_copies:
            copy.start()

    taps = rows
    window = 2 * taps
    reach = taps + RB
    rest = xf.shape[0] - 2 * rows
    xf[pl.ds(2 * rows, rest), :] = jnp.zeros((rest, channels), bf16)
    xb[pl.ds(2 * rows, rest), :] = jnp.zeros((rest, channels), bf16)

    def build(i, carry):
        for which, dest in ((0, hf), (1, hb)):
            tile = base_ref[which, pl.ds(pl.multiple_of(i * groups, groups), groups), :]
            for g in range(groups):
                row = jnp.broadcast_to(tile[g : g + 1, :], (RB, window))
                skew = pltpu.roll(row, 0, 1, stride=1, stride_axis=0)
                dest[pl.ds(pl.multiple_of((i * groups + g) * RB, RB), RB), :] = skew.astype(bf16)
        return carry

    lax.fori_loop(0, channels // LANES, build, 0)

    @pl.when(has_left)
    def _():
        for copy in rim_copies:
            copy.wait_recv()

    @pl.when(jnp.logical_not(has_left))
    def _():
        for rim in (rim_q, rim_k, rim_v):
            rim[...] = jnp.zeros_like(rim)
        xf[pl.ds(0, rows), :] = jnp.zeros((rows, channels), bf16)

    @pl.when(jnp.logical_not(has_right))
    def _():
        xb[pl.ds(rows, rows), :] = jnp.zeros((rows, channels), bf16)
        for rim in (eq, ek, ev):
            rim[pl.ds(rows, PAD), :] = jnp.zeros((PAD, channels), bf16)

    def forward(slot, x_ref, rim, col):
        scr[slot, 0:PAD, :] = rim[:, col].astype(f32)
        scr[slot, PAD : PAD + rows, :] = x_ref[:, col].astype(f32)
        total = taps_ref[slot, 0:1, col] * scr[slot, PAD : PAD + rows, :]
        for j in range(1, short):
            total = total + taps_ref[slot, j : j + 1, col] * (
                mshort_ref[j - 1] * scr[slot, PAD - j : PAD - j + rows, :]
            )
        return total

    def first(i, carry):
        col = lanes_of(i)
        query = forward(0, q_ref, rim_q, col)
        qs[:, col] = query
        xb[0:rows, col] = (d_ref[:, col].astype(f32) * query).astype(bf16)
        key = forward(1, k_ref, rim_k, col)
        ks[:, col] = key
        value = forward(2, v_ref, rim_v, col)
        vs[:, col] = value
        xf[rows : 2 * rows, col] = (key * value).astype(bf16)
        return carry

    gp_copies, cg_copies, eb_copies = [], [], []
    for chunk in range(chunks):
        lo = chunk * steps * LANES
        span = pl.ds(lo, steps * LANES)
        gp_copies.append(remote(
            xf.at[pl.ds(rows, rows), span], xf.at[pl.ds(0, rows), span], gp_ss.at[chunk], gp_rs.at[chunk], right))
        cg_copies.append(remote(
            xb.at[pl.ds(0, rows), span], xb.at[pl.ds(rows, rows), span], cg_ss.at[chunk], cg_rs.at[chunk], left))
        eb_copies.append([
            remote(e.at[pl.ds(0, PAD), span], e.at[pl.ds(rows, PAD), span],
                   eb_ss.at[chunk * 3 + i], eb_rs.at[chunk * 3 + i], left)
            for i, e in enumerate((eq, ek, ev))
        ])

    for chunk in range(chunks):
        lax.fori_loop(chunk * steps, (chunk + 1) * steps, first, 0)

        if chunk < DEPTH:
            @pl.when(has_right)
            def _():
                gp_copies[chunk].start()

            @pl.when(has_left)
            def _():
                cg_copies[chunk].start()

    lane_group = lax.broadcasted_iota(jnp.int32, (RB, LANES), 1) // width

    def diagonal(out):
        y = out[0:RB]
        for g in range(1, groups):
            y = jnp.where(lane_group == g, out[g * RB : (g + 1) * RB], y)
        return y

    def part_copy(owner, sender):
        return remote(parts.at[owner], inbox.at[sender], ps_ss.at[owner], ps_rs.at[sender], (grp, owner))

    def done_copy(owner, peer):
        return remote(done.at[owner], done.at[owner], bc_ss.at[peer], bc_rs.at[owner], (grp, peer))

    def over_peers(act):
        def step(offset, carry):
            act(peer_of(offset))
            return carry

        lax.fori_loop(1, n, step, 0)

    per = parts.shape[1]

    def second(i, carry):
        col = lanes_of(i)
        hrows = pl.ds(pl.multiple_of(i * groups * RB, groups * RB), groups * RB)
        gain = gain_ref[0:1, col]
        total = None
        for a in range(rows // RB):
            own = slice(a * RB, (a + 1) * RB)
            mf = mf_ref[own, :]
            source = xf[a * RB : a * RB + window, col]
            table = (hf[hrows, :].reshape(groups, RB, window) * mf[None]).reshape(groups * RB, window)
            conv = diagonal(jnp.dot(table, source, preferred_element_type=f32))
            pair = xf[rows + a * RB : rows + (a + 1) * RB, col]
            conv = conv + gain * pair.astype(f32)
            so_ref[own, col] = (qs[own, col] * conv).astype(bf16)
            eq[own, col] = (d_ref[own, col].astype(f32) * conv).astype(bf16)
            grad = xb[own, col]
            spread = (grad[None] * lm_ref[...]).reshape(groups * RB, LANES)
            terms = lax.dot_general(
                xf[a * RB : a * RB + reach, col], spread, (((1,), (1,)), ((), ())), preferred_element_type=f32)
            terms = terms * mt_ref[a]
            total = terms if total is None else total + terms
        total = jnp.concatenate([total, jnp.zeros((window - reach, groups * RB), f32)], axis=0)
        total = total.T.reshape(groups, RB, window)
        half = RB // 2
        upper = total[:, half:].reshape(groups * half, window)
        total = total[:, :half].reshape(groups * half, window) + pltpu.roll(upper, window - half, 1)
        sub = lax.broadcasted_iota(jnp.int32, (groups * half, window), 0)
        shift = 1
        while shift < half:
            total = jnp.where((sub & shift) != 0, pltpu.roll(total, window - shift, 1), total)
            shift *= 2
        terms = jnp.sum(total.reshape(groups, half, window), axis=1)
        terms = pltpu.roll(terms, window - 1, 1)
        if per >= groups:
            parts[i * groups // per, pl.ds(pl.multiple_of(i * groups % per, groups), groups), :] = terms[:, :taps]
        else:
            for m in range(groups // per):
                parts[i * (groups // per) + m] = terms[m * per : (m + 1) * per, :taps]
        return carry

    def pairs(i, carry):
        col = lanes_of(i)
        hrows = pl.ds(pl.multiple_of(i * groups * RB, groups * RB), groups * RB)
        gain = gain_ref[0:1, col]
        for a in range(rows // RB):
            own = slice(a * RB, (a + 1) * RB)
            grads = xb[a * RB : a * RB + window, col]
            table = (hb[hrows, :].reshape(groups, RB, window) * mb_ref[own, :][None]).reshape(groups * RB, window)
            back = diagonal(jnp.dot(table, grads, preferred_element_type=f32))
            grad = xb[own, col]
            back = back + gain * grad.astype(f32)
            ek[own, col] = (back * vs[own, col]).astype(bf16)
            ev[own, col] = (back * ks[own, col]).astype(bf16)
        return carry

    for chunk in range(chunks):
        @pl.when(has_left)
        def _():
            gp_copies[chunk].wait_recv()

        if chunk + DEPTH < chunks:
            @pl.when(has_right)
            def _():
                gp_copies[chunk].wait_send()
                gp_copies[chunk + DEPTH].start()

            @pl.when(has_left)
            def _():
                cg_copies[chunk].wait_send()
                cg_copies[chunk + DEPTH].start()

        lax.fori_loop(chunk * steps, (chunk + 1) * steps, second, 0)

        @pl.when(has_left)
        def _():
            eb_copies[chunk][0].start()

    over_peers(lambda peer: part_copy(peer, me).start())

    for chunk in range(chunks):
        @pl.when(has_right)
        def _():
            cg_copies[chunk].wait_recv()

        lax.fori_loop(chunk * steps, (chunk + 1) * steps, pairs, 0)

        @pl.when(has_left)
        def _():
            eb_copies[chunk][1].start()
            eb_copies[chunk][2].start()

        if chunk == chunks // 2 - 1:
            over_peers(lambda peer: part_copy(peer, peer).wait_recv())
            total = parts[me]

            def add(offset, total):
                return total + inbox[peer_of(offset)]

            done[me] = lax.fori_loop(1, n, add, total)
            over_peers(lambda peer: done_copy(me, peer).start())


    def backward(slot, e_ref, out_ref, col):
        scr[slot] = e_ref[:, col].astype(f32)
        total = taps_ref[slot, 0:1, col] * scr[slot, 0:rows, :]
        for j in range(1, short):
            total = total + taps_ref[slot, j : j + 1, col] * (
                mshort_ref[short - 2 + j] * scr[slot, j : j + rows, :]
            )
        out_ref[:, col] = total.astype(bf16)

    def third(i, carry):
        col = lanes_of(i)
        backward(0, eq, gq_ref, col)
        backward(1, ek, gk_ref, col)
        backward(2, ev, gv_ref, col)
        return carry

    for chunk in range(chunks):
        @pl.when(has_right)
        def _():
            for copy in eb_copies[chunk]:
                copy.wait_recv()

        lax.fori_loop(chunk * steps, (chunk + 1) * steps, third, 0)

    @pl.when(has_right)
    def _():
        for copy in rim_copies:
            copy.wait_send()
        for copy in gp_copies[chunks - DEPTH :]:
            copy.wait_send()

    @pl.when(has_left)
    def _():
        for copy in cg_copies[chunks - DEPTH :]:
            copy.wait_send()
        for copies in eb_copies:
            for copy in copies:
                copy.wait_send()

    over_peers(lambda peer: part_copy(peer, peer).wait_send())
    over_peers(lambda peer: done_copy(peer, peer).wait_recv())
    over_peers(lambda peer: done_copy(me, peer).wait_send())
    flip = (
        lax.broadcasted_iota(jnp.int32, (taps, taps), 0) + lax.broadcasted_iota(jnp.int32, (taps, taps), 1)
        == taps - 1
    ).astype(f32)
    f_ref[...] = scale * lax.dot_general(
        flip, done[...].reshape(n * per, taps), (((1,), (1,)), ((), ())),
        precision=lax.Precision.HIGHEST, preferred_element_type=f32)


def body(q, k, v, d, short_taps, long_filter, skip_gain, genome_ids):
    rows, channels = q.shape
    taps, filters = long_filter.shape
    width = channels // filters
    groups = LANES // width
    short = short_taps.shape[1]
    n = lax.axis_size("seq")
    me = lax.axis_index("seq")
    f32, bf16 = jnp.float32, jnp.bfloat16
    window = 2 * taps
    chunks = 8
    ext = 2 * rows + window - RB - rows
    ext = max(ext, 3 * rows - RB)

    padded = jnp.pad(genome_ids, (taps, 2 * taps), constant_values=-1)
    ids = lax.dynamic_slice_in_dim(padded, me * rows, 2 * taps + 2 * rows, 0)
    own = ids[taps : taps + rows]
    blocks = rows // RB
    front = jnp.stack([ids[a * RB : a * RB + window] for a in range(blocks)])
    back = jnp.stack([ids[taps + a * RB : taps + a * RB + window] for a in range(blocks)])
    own_blocks = own.reshape(blocks, RB, 1)
    mf = (own_blocks == front[:, None, :]).astype(bf16).reshape(rows, window)
    mb = (own_blocks == back[:, None, :]).astype(bf16).reshape(rows, window)
    same_t = (own.reshape(blocks, 1, RB) == front[:, : taps + RB, None]).astype(f32)
    mt = jnp.tile(same_t, (1, 1, groups))
    mshort = jnp.stack(
        [own == ids[taps - j : taps - j + rows] for j in range(1, short)]
        + [own == ids[taps + j : taps + j + rows] for j in range(1, short)]
    ).astype(f32)
    mshort = jnp.broadcast_to(mshort[:, :, None], (2 * (short - 1), rows, LANES))
    filt = long_filter.astype(f32).T
    base = jnp.stack([
        jnp.pad(filt[:, ::-1], ((0, 0), (1, window - taps - 1))),
        jnp.pad(filt, ((0, 0), (0, window - taps))),
    ])
    lane = lax.broadcasted_iota(jnp.int32, (groups, RB, LANES), 2) // width
    lm = (lane == lax.broadcasted_iota(jnp.int32, (groups, RB, LANES), 0)).astype(bf16)

    scale = 1.0 / math.sqrt(width * rows * n)
    big = jax.ShapeDtypeStruct((rows, channels), bf16)
    vm = pl.BlockSpec(memory_space=pltpu.VMEM)
    dma = pltpu.SemaphoreType.DMA
    so, gq, gk, gv, terms = pl.pallas_call(
        functools.partial(kernel, n, chunks, width, scale),
        out_shape=(big, big, big, big, jax.ShapeDtypeStruct((taps, filters), f32)),
        in_specs=[vm] * 12,
        out_specs=(vm,) * 5,
        scratch_shapes=[
            pltpu.VMEM((PAD, channels), bf16),
            pltpu.VMEM((PAD, channels), bf16),
            pltpu.VMEM((PAD, channels), bf16),
            pltpu.VMEM((ext, channels), bf16),
            pltpu.VMEM((ext, channels), bf16),
            pltpu.VMEM((rows, channels), f32),
            pltpu.VMEM((rows, channels), f32),
            pltpu.VMEM((rows, channels), f32),
            pltpu.VMEM((filters * RB, window), bf16),
            pltpu.VMEM((filters * RB, window), bf16),
            pltpu.VMEM((rows + PAD, channels), bf16),
            pltpu.VMEM((rows + PAD, channels), bf16),
            pltpu.VMEM((rows + PAD, channels), bf16),
            pltpu.VMEM((3, rows + PAD, LANES), f32),
            pltpu.VMEM((n, filters // n, taps), f32),
            pltpu.VMEM((n, filters // n, taps), f32),
            pltpu.VMEM((n, filters // n, taps), f32),
            dma((3,)), dma((3,)),
            dma((chunks,)), dma((chunks,)),
            dma((chunks,)), dma((chunks,)),
            dma((3 * chunks,)), dma((3 * chunks,)),
            dma((n,)), dma((n,)), dma((n,)), dma((n,)),
        ],
        compiler_params=pltpu.CompilerParams(
            collective_id=0, has_side_effects=True, vmem_limit_bytes=56 * 1024 * 1024
        ),
    )(q, k, v, d, short_taps, base, skip_gain.reshape(1, channels), mshort, mf, mb, lm, mt)
    return so, gq, gk, gv, terms


def solution(mesh):
    tile = P(("grp", "seq"), None)
    return jax.shard_map(
        body,
        mesh=mesh,
        in_specs=(tile, tile, tile, tile, P(), P(), P(), P("grp")),
        out_specs=(tile, tile, tile, tile, P("grp", None)),
        check_vma=False,
    )
```
